32 devices in a mesh: groups: 2 (over x), walk: 16 (over z, y, core).
Axes of the slice: x: 2, y: 2, z: 4, core: 2. Of those that a mesh axis runs over, the one named last changes fastest.
Arguments:
- walkers: bfloat16 [32, 768, 1536], P(('groups', 'walk')), parts along dimension 0, may hold values from -6 to 6
- theta: bfloat16 [32, 768, 1536], P(('groups', 'walk')), parts along dimension 0, may hold values from -0.21875 to 0.21875
- cholesky: float32 [32, 16, 4, 4096], P(('groups', 'walk')), parts along dimension 0, may hold values from -0.875 to 0.875
- tiles: int32 [32, 4], P('groups'), parts along dimension 0, may hold values from 0 to 575, as said below
- fields: float32 [2, 32, 256], P(None, ('groups', 'walk')), parts along dimension 1, may hold values from -5 to 5
- source: int32 [32], P('groups'), parts along dimension 0, may hold values from 0 to 15
Outputs:
- walkers_out: bfloat16 [32, 768, 1536], P(('groups', 'walk')), parts along dimension 0
- force_bias: float32 [2, 32, 256], P(None, ('groups', 'walk')), parts along dimension 1
The draws below stay inside these ranges and needn't reach their ends.
There are 2 independent parts, one for each index of `groups`. The reference program is written for one: setup_inputs(seed, part) draws one part's arguments, and reference() takes and returns one part's arrays. A program takes and returns all parts, laid end to end along the dimension named above; each array names one. Nothing has to cross between parts.
Inputs may be any that keep to these rules, and one draw needn't show every extreme that they name: `tiles`: the 4 tile ids of one block are distinct.
All inputs are finite; a program needn't handle non-finite values.
Results may differ from the reference program's by a relative error of at most 0.0065.
Values may be sent and summed in bfloat16 or wider, within the bound.
A program may use at most 128 MiB of HBM per device.

```python
import jax
import jax.numpy as jnp
from jax import lax

NORB = 1536
NOCC = 768
TILE = 64
NT = 4
CDEV = 16
NBLK = 16
NCHOL = 256
WALKERS = 16


def pick_row(one_key):
    return jax.random.permutation(one_key, (NORB // TILE) ** 2)[:NT].astype(jnp.int32)


def draw_tiles(key, part):
    key = jax.random.fold_in(key, 7)
    count = (NORB // TILE) ** 2
    keys = jax.random.split(key, NBLK + 2)
    rows = jax.vmap(pick_row)(keys[:NBLK])
    chosen_block = jax.random.randint(keys[NBLK], (), 0, NBLK)
    inner = (jax.random.permutation(keys[NBLK + 1], count - 2)[:NT - 2] + 1).astype(jnp.int32)
    special = jnp.concatenate([jnp.array([0, count - 1], jnp.int32), inner])
    hit = (jnp.arange(NBLK) == chosen_block)[:, None]
    return jnp.where(hit, special[None, :], rows)


def plant(values, rng, low, top_value):
    extent = values.shape
    place = [jax.random.randint(jax.random.fold_in(rng, axis), (), 0, extent[axis]) for axis in range(len(extent))]
    values = values.at[tuple(place)].set(low)
    longest = extent.index(max(extent))
    place[longest] = (place[longest] + 1) % extent[longest]
    return values.at[tuple(place)].set(top_value)


def block_scale(rng, dims, shards, smallest, top_value):
    level, own = 1.0, jax.random.fold_in(rng, 6)
    for dim, parts in shards:
        draws = jnp.exp(jax.random.uniform(jax.random.fold_in(own, dim), (parts,), jnp.float32, smallest / len(shards), top_value / len(shards)))
        level = level * jnp.repeat(draws, dims[dim] // parts).reshape([-1 if axis == dim else 1 for axis in range(len(dims))])
    return level


def scatter_about(stream_key, dims, scale, bound, cuts=(), held_as=jnp.bfloat16):
    gain = block_scale(stream_key, dims, cuts, -0.22, 0.18) if cuts else 1.0
    values = jax.random.normal(stream_key, dims, jnp.float32) * scale * gain
    return jnp.minimum(jnp.maximum(values, -bound), bound).astype(held_as)


def setup_inputs(seed: int = 0, part: int = 0) -> dict:
    splits = jax.random.split(jax.random.key(seed), 7)
    part_splits = jax.random.split(jax.random.fold_in(splits[6], part), 7)
    walkers = scatter_about(part_splits[0], (WALKERS, NOCC, NORB), 1.0, 6.0, ((0, 16),))
    theta = scatter_about(part_splits[1], (WALKERS, NOCC, NORB), NOCC ** -0.5, 0.21875, ((0, 16),))
    cholesky = scatter_about(part_splits[2], (NBLK, CDEV, NT, TILE * TILE), (3 * (NCHOL * NT * TILE * TILE // NORB) ** -0.5), 0.875, ((0, 16),), jnp.float32)
    tiles = draw_tiles(jax.random.fold_in(jax.random.fold_in(splits[6], part), 71), part)
    fields = scatter_about(part_splits[4], (2, WALKERS, NCHOL), 1.0, 5.0, ((1, 16),), jnp.float32)
    source = plant(jax.random.randint(part_splits[5], (WALKERS,), 0, WALKERS), jax.random.fold_in(part_splits[5], 1), 0, WALKERS - 1).astype(jnp.int32)
    return dict(walkers=walkers, theta=theta, cholesky=cholesky, tiles=tiles, fields=fields, source=source)


def reference(walkers, theta, cholesky, tiles, fields, source):
    tile_rows = NORB // TILE
    flat_ids = tiles.reshape(-1).astype(jnp.int32)
    chol_flat = cholesky.reshape(NBLK, CDEV, NT * TILE * TILE)
    orbitals = walkers
    collected = []
    for sweep in range(2):
        def green_pick(pair):
            panel, current = pair
            green = jnp.dot(panel.astype(jnp.float32).T, current.astype(jnp.float32), precision=lax.Precision.HIGHEST).astype(jnp.bfloat16)
            green = green.reshape(tile_rows, TILE, tile_rows, TILE).transpose(0, 2, 1, 3).reshape(tile_rows * tile_rows, TILE * TILE)
            return green[flat_ids].reshape(NBLK, NT * TILE * TILE)

        picked = lax.map(green_pick, (theta, orbitals))
        per_block = jnp.transpose(picked, (1, 0, 2))

        def block_bias(pair):
            green_block, chol_block = pair
            return jnp.dot(green_block.astype(jnp.float32), chol_block.T, precision=lax.Precision.HIGHEST)

        bias = lax.map(block_bias, (per_block, chol_flat))
        bias = jnp.transpose(bias, (1, 0, 2)).reshape(WALKERS, NCHOL)
        collected.append(bias)
        shift = fields[sweep] - jnp.clip(0.5 * bias, -1.0, 1.0)
        shift_blocks = jnp.transpose(shift.reshape(WALKERS, NBLK, CDEV), (1, 0, 2))

        def block_partial(pair):
            shift_block, chol_block = pair
            return (0.1 * jnp.dot(shift_block, chol_block, precision=lax.Precision.HIGHEST)).astype(jnp.bfloat16)

        partial_value = lax.map(block_partial, (shift_blocks, chol_flat))
        partial_value = jnp.transpose(partial_value, (1, 0, 2)).reshape(WALKERS, NBLK * NT, TILE * TILE)

        def advance(pair):
            current, pieces = pair
            potential = jnp.zeros((tile_rows * tile_rows, TILE * TILE), jnp.float32).at[flat_ids].add(pieces.astype(jnp.float32))
            potential = potential.astype(jnp.bfloat16).reshape(tile_rows, tile_rows, TILE, TILE).transpose(0, 2, 1, 3).reshape(NORB, NORB)
            moved = jnp.dot(current.astype(jnp.float32), potential.astype(jnp.float32), precision=lax.Precision.HIGHEST)
            return (current.astype(jnp.float32) + moved).astype(jnp.bfloat16)

        orbitals = lax.map(advance, (orbitals, partial_value))
    walkers_out = orbitals[source.astype(jnp.int32)]
    return walkers_out, jnp.stack(collected)
```

```python
import functools

import jax
import jax.numpy as jnp
from jax import lax
from jax.experimental import pallas as pl
from jax.experimental.pallas import tpu as pltpu
from jax.sharding import PartitionSpec as P

TILE = 64
LANES = 128
CHUNK = 256
VMEM_LIMIT = 52 * 1024 * 1024


def half_mask(rows):
    return lax.broadcasted_iota(jnp.int32, (rows, LANES), 1) < TILE


def pick_tile(green, row, col, odd):
    chunk = green[pl.ds(pl.multiple_of(row, TILE), TILE), pl.ds(pl.multiple_of(col, LANES), LANES)]
    chunk = chunk.astype(jnp.float32)
    low = lax.broadcasted_iota(jnp.int32, chunk.shape, 1) < TILE
    keep = low == (odd == 0)
    return jnp.where(keep, chunk, pltpu.roll(chunk, TILE, 1))


def add_tile(potential, row, col, odd, shift, block):
    total = shift[0:1] * block[0].astype(jnp.float32)
    for pair in range(1, len(block)):
        total = total + shift[pair : pair + 1] * block[pair].astype(jnp.float32)
    total = total + pltpu.roll(total, TILE, 1)
    total = (0.1 * total).astype(jnp.bfloat16).astype(jnp.float32)
    low = lax.broadcasted_iota(jnp.int32, total.shape, 1) < TILE
    keep = low == (odd == 0)
    at = (pl.ds(pl.multiple_of(row, TILE), TILE), pl.ds(pl.multiple_of(col, LANES), LANES))
    potential[at] = potential[at] + jnp.where(keep, total, 0.0)


def step_kernel(move, rows_ref, cols_ref, odds_ref, theta_t, orbitals, chol, fields, *rest):
    if move:
        bias_ref, shift_ref, out, green, potential = rest
    else:
        bias_ref, shift_ref, green = rest
    now = pl.program_id(0)
    blocks, pairs, slots = chol.shape[:3]
    width = orbitals.shape[1]

    @pl.when(now == 0)
    def _():
        @pl.loop(0, width // CHUNK)
        def _(i):
            at = pl.ds(pl.multiple_of(i * CHUNK, CHUNK), CHUNK)
            green[:, at] = jnp.dot(
                theta_t[...], orbitals[:, at], preferred_element_type=jnp.float32
            ).astype(green.dtype)
            if move:
                potential[:, at] = jnp.zeros((potential.shape[0], CHUNK), jnp.float32)

    @pl.loop(0, blocks)
    def _(b):
        base = (now * blocks + b) * slots
        acc = [jnp.zeros((8, LANES), jnp.float32) for _ in range(pairs)]
        for t in range(slots):
            g = pick_tile(green, rows_ref[base + t], cols_ref[base + t], odds_ref[base + t])
            for pair in range(pairs):
                product = g * chol[b, pair, t].astype(jnp.float32)
                acc[pair] = acc[pair] + jnp.sum(product.reshape(TILE // 8, 8, LANES), axis=0)
        sums = jnp.concatenate([jnp.sum(a, axis=0, keepdims=True) for a in acc], axis=0)
        low = half_mask(pairs)
        first = jnp.sum(jnp.where(low, sums, 0.0), axis=1, keepdims=True)
        second = jnp.sum(jnp.where(low, 0.0, sums), axis=1, keepdims=True)
        bias = jnp.where(low, first, second)
        shift = fields[b] - jnp.clip(0.5 * bias, -1.0, 1.0)
        bias_ref[b] = bias
        shift_ref[b] = shift
        if move:
            for t in range(slots):
                add_tile(
                    potential, rows_ref[base + t], cols_ref[base + t], odds_ref[base + t],
                    shift, [chol[b, pair, t] for pair in range(pairs)],
                )

    if move:
        @pl.when(now == pl.num_programs(0) - 1)
        def _():
            @pl.loop(0, width // CHUNK)
            def _(i):
                at = pl.ds(pl.multiple_of(i * CHUNK, CHUNK), CHUNK)
                moved = jnp.dot(
                    orbitals[...], potential[:, at].astype(jnp.bfloat16),
                    preferred_element_type=jnp.float32,
                )
                out[:, at] = (orbitals[:, at].astype(jnp.float32) + moved).astype(out.dtype)


def potential_kernel(rows_ref, cols_ref, odds_ref, chol, shifts, out1, out2, one, two):
    now = pl.program_id(0)
    blocks, pairs, slots = chol.shape[:3]
    width = one.shape[1]

    @pl.when(now == 0)
    def _():
        @pl.loop(0, width // CHUNK)
        def _(i):
            at = pl.ds(pl.multiple_of(i * CHUNK, CHUNK), CHUNK)
            one[:, at] = jnp.zeros((one.shape[0], CHUNK), jnp.float32)
            two[:, at] = jnp.zeros((two.shape[0], CHUNK), jnp.float32)

    @pl.loop(0, blocks)
    def _(b):
        base = (now * blocks + b) * slots
        for t in range(slots):
            block = [chol[b, pair, t] for pair in range(pairs)]
            place = (rows_ref[base + t], cols_ref[base + t], odds_ref[base + t])
            add_tile(one, *place, shifts[0, b], block)
            add_tile(two, *place, shifts[1, b], block)

    @pl.when(now == pl.num_programs(0) - 1)
    def _():
        @pl.loop(0, width // CHUNK)
        def _(i):
            at = pl.ds(pl.multiple_of(i * CHUNK, CHUNK), CHUNK)
            out1[:, at] = one[:, at].astype(out1.dtype)
            out2[:, at] = two[:, at].astype(out2.dtype)


def moves_kernel(orbitals, first, second, out, mid):
    width = orbitals.shape[1]

    def move(source, potential, target):
        @pl.loop(0, width // CHUNK)
        def _(i):
            at = pl.ds(pl.multiple_of(i * CHUNK, CHUNK), CHUNK)
            moved = jnp.dot(source[...], potential[:, at], preferred_element_type=jnp.float32)
            target[:, at] = (source[:, at].astype(jnp.float32) + moved).astype(target.dtype)

    move(orbitals, first, mid)
    move(mid, second, out)


def whole(shape):
    return pl.BlockSpec(shape, lambda i, *_: (0,) * len(shape), pipeline_mode=pl.Buffered(1))


def step(move, places, theta_t, orbitals, chol, fields):
    count, pairs, slots = chol.shape[:3]
    occupied, width = orbitals.shape
    per = 4 if count % 4 == 0 else 1
    lanes = pl.BlockSpec((per, pairs, LANES), lambda i, *_: (i, 0, 0))
    small = jax.ShapeDtypeStruct((count, pairs, LANES), jnp.float32)
    flops = 2 * occupied * width * width * (2 if move else 1)
    return pl.pallas_call(
        functools.partial(step_kernel, move),
        out_shape=(small, small) + ((jax.ShapeDtypeStruct((occupied, width), jnp.bfloat16),) if move else ()),
        grid_spec=pltpu.PrefetchScalarGridSpec(
            num_scalar_prefetch=3,
            grid=(count // per,),
            in_specs=[
                whole((width, occupied)),
                whole((occupied, width)),
                pl.BlockSpec((per, pairs, slots, TILE, LANES), lambda i, *_: (i, 0, 0, 0, 0)),
                lanes,
            ],
            out_specs=(lanes, lanes) + ((whole((occupied, width)),) if move else ()),
            scratch_shapes=[pltpu.VMEM((width, width), jnp.bfloat16)]
            + ([pltpu.VMEM((width, width), jnp.float32)] if move else []),
        ),
        compiler_params=pltpu.CompilerParams(vmem_limit_bytes=VMEM_LIMIT),
        cost_estimate=pl.CostEstimate(flops=flops, bytes_accessed=2 * chol.size, transcendentals=0),
        name="step",
    )(*places, theta_t, orbitals, chol, fields)


def potentials(places, chol, shifts, width):
    count, pairs, slots = chol.shape[:3]
    per = 4 if count % 4 == 0 else 1
    full = jax.ShapeDtypeStruct((width, width), jnp.bfloat16)
    return pl.pallas_call(
        potential_kernel,
        out_shape=(full, full),
        grid_spec=pltpu.PrefetchScalarGridSpec(
            num_scalar_prefetch=3,
            grid=(count // per,),
            in_specs=[
                pl.BlockSpec((per, pairs, slots, TILE, LANES), lambda i, *_: (i, 0, 0, 0, 0)),
                pl.BlockSpec((2, per, pairs, LANES), lambda i, *_: (0, i, 0, 0)),
            ],
            out_specs=(whole((width, width)),) * 2,
            scratch_shapes=[pltpu.VMEM((width, width), jnp.float32)] * 2,
        ),
        compiler_params=pltpu.CompilerParams(vmem_limit_bytes=VMEM_LIMIT),
        cost_estimate=pl.CostEstimate(flops=4 * chol.size, bytes_accessed=2 * chol.size, transcendentals=0),
        name="potentials",
    )(*places, chol, shifts)


def moves(orbitals, first, second):
    occupied, width = orbitals.shape
    vmem = pl.BlockSpec(memory_space=pltpu.VMEM)
    return pl.pallas_call(
        moves_kernel,
        out_shape=jax.ShapeDtypeStruct((occupied, width), jnp.bfloat16),
        in_specs=[vmem] * 3,
        out_specs=vmem,
        scratch_shapes=[pltpu.VMEM((occupied, width), jnp.bfloat16)],
        compiler_params=pltpu.CompilerParams(vmem_limit_bytes=VMEM_LIMIT),
        cost_estimate=pl.CostEstimate(
            flops=4 * occupied * width * width, bytes_accessed=4 * width * width, transcendentals=0
        ),
        name="moves",
    )(orbitals, first, second)


def spread(values, vectors):
    lead = values.shape[:-1]
    shaped = values.reshape(*lead, -1, vectors // 2, 2, 1)
    return jnp.broadcast_to(shaped, (*shaped.shape[:-1], TILE)).reshape(*shaped.shape[:-2], LANES)


def local(walkers, theta, cholesky, tiles, fields, source):
    own_walkers, occupied, width = walkers.shape
    tile_rows = width // TILE
    vectors, slots = cholesky.shape[1:3]

    halves = cholesky[0].astype(jnp.bfloat16).reshape(vectors // 2, 2, slots, TILE, TILE)
    halves = jnp.transpose(halves, (0, 2, 3, 1, 4)).reshape(vectors // 2, slots, TILE, LANES)
    chol = lax.all_gather(halves, "walk", axis=0, tiled=False)

    shares = lax.all_to_all(walkers, "walk", split_axis=1, concat_axis=0, tiled=True)
    chosen = jnp.take(shares, source, axis=0, mode="clip")
    origin = lax.all_to_all(chosen, "walk", split_axis=0, concat_axis=1, tiled=True)[0]

    flat = tiles.reshape(-1)
    row, col = flat // tile_rows, flat % tile_rows
    places = (row * TILE, (col // 2) * LANES, col % 2)
    theta_t = theta[0].T
    drive = spread(fields[:, 0], vectors)
    bias1, shift1, orbitals = step(True, places, theta_t, walkers[0], chol, drive[0])
    bias2, shift2 = step(False, places, theta_t, orbitals, chol, drive[1])
    biases = jnp.stack([bias1, bias2])[..., ::TILE].reshape(2, 1, -1)
    own_shift = jnp.stack([shift1, shift2])[..., ::TILE].reshape(2, -1)
    all_shifts = lax.all_gather(own_shift, "walk", axis=0, tiled=False)
    me = lax.axis_index("walk")
    mine = lax.dynamic_index_in_dim(source, me, 0, keepdims=False)
    chosen_shift = lax.dynamic_index_in_dim(all_shifts, mine, 0, keepdims=False)
    first, second = potentials(places, chol, spread(chosen_shift, vectors), width)
    return (moves(origin, first, second)[None], biases)


def solution(mesh):
    in_specs = (
        P(("groups", "walk"), None, None),
        P(("groups", "walk"), None, None),
        P(("groups", "walk"), None, None, None),
        P("groups", None),
        P(None, ("groups", "walk"), None),
        P("groups"),
    )
    out_specs = (P(("groups", "walk"), None, None), P(None, ("groups", "walk"), None))
    return jax.shard_map(local, mesh=mesh, in_specs=in_specs, out_specs=out_specs, check_vma=False)
```

```python
import functools

import jax
import jax.numpy as jnp
from jax import lax
from jax.experimental import pallas as pl
from jax.experimental.pallas import tpu as pltpu
from jax.sharding import PartitionSpec as P

MESH = pl.DeviceIdType.MESH
TILE = 64
LANES = 128
CHUNK = 256
VMEM_LIMIT = 52 * 1024 * 1024


def plane(count):
    chips = count // 2
    short = 1
    while (2 * short) * (2 * short) <= chips and chips % (2 * short) == 0:
        short *= 2
    return chips // short, short


def greet(count, me):
    barrier = pltpu.get_barrier_semaphore()

    @pl.loop(1, count)
    def _(k):
        pl.semaphore_signal(
            barrier, inc=1, device_id={"walk": lax.rem(me + k, count)}, device_id_type=MESH
        )

    pl.semaphore_wait(barrier, count - 1)


def exchange_kernel(count, own, rows, blocks, shares, own_sem, send, recv, row_send, row_recv):
    long, short = plane(count)
    me = lax.axis_index("walk")
    core = lax.rem(me, 2)
    y = lax.rem(me // 2, short)
    z = me // (2 * short)

    def index(a, b, c):
        return (a * short + b) * 2 + c

    def hop(source, slot, way, target):
        return pltpu.make_async_remote_copy(
            src_ref=source, dst_ref=blocks.at[slot], send_sem=send.at[way, slot],
            recv_sem=recv.at[slot], device_id={"walk": target}, device_id_type=MESH,
        )

    def row_copy(k):
        target = lax.rem(me + k, count)
        return pltpu.make_async_remote_copy(
            src_ref=rows.at[target], dst_ref=shares.at[me], send_sem=row_send.at[k],
            recv_sem=row_recv.at[k], device_id={"walk": target}, device_id_type=MESH,
        )

    def ways(dz, dy):
        line = dy == 0
        return (
            (0, line & (dz <= 0) & (z < long - 1), index(z + 1, y, core)),
            (1, line & (dz >= 0) & (z > 0), index(z - 1, y, core)),
            (2, (dy <= 0) & (y < short - 1), index(z, y + 1, core)),
            (3, (dy >= 0) & (y > 0), index(z, y - 1, core)),
        )

    def signed(k):
        return jnp.where(lax.rem(k, 2) == 1, (k + 1) // 2, -(k // 2))

    spread_z, spread_y = 2 * long - 1, 2 * short - 1
    greet(count, me)

    for way, whether, target in ways(0, 0):
        @pl.when(whether)
        def _(way=way, target=target):
            hop(own, me, way, target).start()
    hop(own, me, 4, index(z, y, 1 - core)).start()

    @pl.loop(1, count)
    def _(k):
        row_copy(k).start()

    keep = pltpu.make_async_copy(own, blocks.at[me], own_sem.at[0])
    keep_rows = pltpu.make_async_copy(rows.at[me], shares.at[me], own_sem.at[1])
    keep.start()
    keep_rows.start()

    def each(act, start):
        @pl.loop(start, spread_z * spread_y)
        def _(k):
            dy, dz = signed(k // spread_z), signed(lax.rem(k, spread_z))
            inside = (z + dz >= 0) & (z + dz < long) & (y + dy >= 0) & (y + dy < short)

            @pl.when(inside)
            def _():
                act(dz, dy, index(z + dz, y + dy, core))

    def forward(dz, dy, slot):
        hop(own, slot, 0, index(z, y, 1 - core)).wait_recv()
        for way, whether, target in ways(dz, dy):
            @pl.when(whether)
            def _(way=way, target=target):
                hop(blocks.at[slot], slot, way, target).start()
        hop(blocks.at[slot], slot, 4, index(z, y, 1 - core)).start()

    def finish(dz, dy, slot):
        for way, whether, target in ways(dz, dy):
            @pl.when(whether)
            def _(way=way, target=target):
                hop(own, slot, way, target).wait_send()
        hop(own, slot, 4, index(z, y, 1 - core)).wait_send()
        other = slot + 1 - 2 * core
        hop(own, other, 4, index(z, y, 1 - core)).wait_recv()

    each(forward, 1)
    each(finish, 0)
    keep.wait()
    keep_rows.wait()

    @pl.loop(1, count)
    def _(k):
        row_copy(k).wait()


def exchange(own, rows):
    count = rows.shape[0]
    anywhere = pl.BlockSpec(memory_space=pl.ANY)
    return pl.pallas_call(
        functools.partial(exchange_kernel, count),
        out_shape=(
            jax.ShapeDtypeStruct((count, *own.shape), own.dtype),
            jax.ShapeDtypeStruct(rows.shape, rows.dtype),
        ),
        in_specs=[anywhere] * 2,
        out_specs=(anywhere,) * 2,
        scratch_shapes=[
            pltpu.SemaphoreType.DMA((2,)),
            pltpu.SemaphoreType.DMA((5, count)),
            pltpu.SemaphoreType.DMA((count,)),
            pltpu.SemaphoreType.DMA((count,)),
            pltpu.SemaphoreType.DMA((count,)),
        ],
        compiler_params=pltpu.CompilerParams(collective_id=0, has_side_effects=True),
        name="exchange",
    )(own, rows)


def shifts_kernel(count, own, every, own_sem, send, recv):
    me = lax.axis_index("walk")

    def copy(k):
        return pltpu.make_async_remote_copy(
            src_ref=own, dst_ref=every.at[me], send_sem=send.at[k], recv_sem=recv.at[k],
            device_id={"walk": lax.rem(me + k, count)}, device_id_type=MESH,
        )

    greet(count, me)

    @pl.loop(1, count)
    def _(k):
        copy(k).start()

    keep = pltpu.make_async_copy(own, every.at[me], own_sem)
    keep.start()
    keep.wait()

    @pl.loop(1, count)
    def _(k):
        copy(k).wait()


def gather_shifts(own, count):
    vmem = pl.BlockSpec(memory_space=pltpu.VMEM)
    return pl.pallas_call(
        functools.partial(shifts_kernel, count),
        out_shape=jax.ShapeDtypeStruct((count, *own.shape), own.dtype),
        in_specs=[vmem],
        out_specs=vmem,
        scratch_shapes=[
            pltpu.SemaphoreType.DMA,
            pltpu.SemaphoreType.DMA((count,)),
            pltpu.SemaphoreType.DMA((count,)),
        ],
        compiler_params=pltpu.CompilerParams(collective_id=1, has_side_effects=True),
        name="gather_shifts",
    )(own)


def half_mask(rows):
    return lax.broadcasted_iota(jnp.int32, (rows, LANES), 1) < TILE


def pick_tile(green, row, col, odd):
    chunk = green[pl.ds(pl.multiple_of(row, TILE), TILE), pl.ds(pl.multiple_of(col, LANES), LANES)]
    chunk = chunk.astype(jnp.float32)
    low = lax.broadcasted_iota(jnp.int32, chunk.shape, 1) < TILE
    keep = low == (odd == 0)
    return jnp.where(keep, chunk, pltpu.roll(chunk, TILE, 1))


def add_tile(potential, row, col, odd, shift, block):
    total = shift[0:1] * block[0].astype(jnp.float32)
    for pair in range(1, len(block)):
        total = total + shift[pair : pair + 1] * block[pair].astype(jnp.float32)
    total = total + pltpu.roll(total, TILE, 1)
    total = (0.1 * total).astype(jnp.bfloat16).astype(jnp.float32)
    low = lax.broadcasted_iota(jnp.int32, total.shape, 1) < TILE
    keep = low == (odd == 0)
    at = (pl.ds(pl.multiple_of(row, TILE), TILE), pl.ds(pl.multiple_of(col, LANES), LANES))
    potential[at] = potential[at] + jnp.where(keep, total, 0.0)


def step_kernel(move, rows_ref, cols_ref, odds_ref, theta_t, orbitals, chol, fields, *rest):
    if move:
        bias_ref, shift_ref, out, green, sums, potential = rest
    else:
        bias_ref, shift_ref, green, sums = rest
    now = pl.program_id(0)
    blocks, pairs, slots = chol.shape[:3]
    width = orbitals.shape[1]

    @pl.when(now == 0)
    def _():
        @pl.loop(0, width // CHUNK)
        def _(i):
            at = pl.ds(pl.multiple_of(i * CHUNK, CHUNK), CHUNK)
            green[:, at] = jnp.dot(
                theta_t[...], orbitals[:, at], preferred_element_type=jnp.float32
            ).astype(green.dtype)
            if move:
                potential[:, at] = jnp.zeros((potential.shape[0], CHUNK), jnp.float32)

    for b in range(blocks):
        base = (now * blocks + b) * slots
        acc = [jnp.zeros((8, LANES), jnp.float32) for _ in range(pairs)]
        for t in range(slots):
            g = pick_tile(green, rows_ref[base + t], cols_ref[base + t], odds_ref[base + t])
            for pair in range(pairs):
                product = g * chol[b, pair, t].astype(jnp.float32)
                acc[pair] = acc[pair] + jnp.sum(product.reshape(TILE // 8, 8, LANES), axis=0)
        for pair in range(pairs):
            sums[b, pair] = acc[pair]
    rows = jnp.sum(sums[...], axis=2).reshape(blocks * pairs, LANES)
    low = half_mask(blocks * pairs)
    first = jnp.sum(jnp.where(low, rows, 0.0), axis=1, keepdims=True)
    second = jnp.sum(jnp.where(low, 0.0, rows), axis=1, keepdims=True)
    bias = jnp.where(low, first, second).reshape(blocks, pairs, LANES)
    bias_ref[...] = bias
    shift_ref[...] = fields[...] - jnp.clip(0.5 * bias, -1.0, 1.0)
    if move:
        for b in range(blocks):
            base = (now * blocks + b) * slots
            shift = shift_ref[b]
            for t in range(slots):
                add_tile(
                    potential, rows_ref[base + t], cols_ref[base + t], odds_ref[base + t],
                    shift, [chol[b, pair, t] for pair in range(pairs)],
                )

    if move:
        @pl.when(now == pl.num_programs(0) - 1)
        def _():
            @pl.loop(0, width // CHUNK)
            def _(i):
                at = pl.ds(pl.multiple_of(i * CHUNK, CHUNK), CHUNK)
                moved = jnp.dot(
                    orbitals[...], potential[:, at].astype(jnp.bfloat16),
                    preferred_element_type=jnp.float32,
                )
                out[:, at] = (orbitals[:, at].astype(jnp.float32) + moved).astype(out.dtype)


def potential_kernel(rows_ref, cols_ref, odds_ref, chol, shifts, out1, out2, one, two):
    now = pl.program_id(0)
    blocks, pairs, slots = chol.shape[:3]
    width = one.shape[1]

    @pl.when(now == 0)
    def _():
        @pl.loop(0, width // CHUNK)
        def _(i):
            at = pl.ds(pl.multiple_of(i * CHUNK, CHUNK), CHUNK)
            one[:, at] = jnp.zeros((one.shape[0], CHUNK), jnp.float32)
            two[:, at] = jnp.zeros((two.shape[0], CHUNK), jnp.float32)

    @pl.loop(0, blocks)
    def _(b):
        base = (now * blocks + b) * slots
        for t in range(slots):
            block = [chol[b, pair, t] for pair in range(pairs)]
            place = (rows_ref[base + t], cols_ref[base + t], odds_ref[base + t])
            add_tile(one, *place, shifts[0, b], block)
            add_tile(two, *place, shifts[1, b], block)

    @pl.when(now == pl.num_programs(0) - 1)
    def _():
        @pl.loop(0, width // CHUNK)
        def _(i):
            at = pl.ds(pl.multiple_of(i * CHUNK, CHUNK), CHUNK)
            out1[:, at] = one[:, at].astype(out1.dtype)
            out2[:, at] = two[:, at].astype(out2.dtype)


def moves_kernel(orbitals, first, second, out, mid):
    width = orbitals.shape[1]

    def move(source, potential, target):
        @pl.loop(0, width // CHUNK)
        def _(i):
            at = pl.ds(pl.multiple_of(i * CHUNK, CHUNK), CHUNK)
            moved = jnp.dot(source[...], potential[:, at], preferred_element_type=jnp.float32)
            target[:, at] = (source[:, at].astype(jnp.float32) + moved).astype(target.dtype)

    move(orbitals, first, mid)
    move(mid, second, out)


def whole(shape):
    return pl.BlockSpec(shape, lambda i, *_: (0,) * len(shape), pipeline_mode=pl.Buffered(1))


def step(move, places, theta_t, orbitals, chol, fields):
    count, pairs, slots = chol.shape[:3]
    occupied, width = orbitals.shape
    per = 4 if count % 4 == 0 else 1
    lanes = pl.BlockSpec((per, pairs, LANES), lambda i, *_: (i, 0, 0))
    small = jax.ShapeDtypeStruct((count, pairs, LANES), jnp.float32)
    flops = 2 * occupied * width * width * (2 if move else 1)
    return pl.pallas_call(
        functools.partial(step_kernel, move),
        out_shape=(small, small) + ((jax.ShapeDtypeStruct((occupied, width), jnp.bfloat16),) if move else ()),
        grid_spec=pltpu.PrefetchScalarGridSpec(
            num_scalar_prefetch=3,
            grid=(count // per,),
            in_specs=[
                whole((width, occupied)),
                whole((occupied, width)),
                pl.BlockSpec((per, pairs, slots, TILE, LANES), lambda i, *_: (i, 0, 0, 0, 0)),
                lanes,
            ],
            out_specs=(lanes, lanes) + ((whole((occupied, width)),) if move else ()),
            scratch_shapes=[
                pltpu.VMEM((width, width), jnp.bfloat16),
                pltpu.VMEM((per, pairs, 8, LANES), jnp.float32),
            ]
            + ([pltpu.VMEM((width, width), jnp.float32)] if move else []),
        ),
        compiler_params=pltpu.CompilerParams(vmem_limit_bytes=VMEM_LIMIT),
        cost_estimate=pl.CostEstimate(flops=flops, bytes_accessed=2 * chol.size, transcendentals=0),
        name="step",
    )(*places, theta_t, orbitals, chol, fields)


def potentials(places, chol, shifts, width):
    count, pairs, slots = chol.shape[:3]
    per = 4 if count % 4 == 0 else 1
    full = jax.ShapeDtypeStruct((width, width), jnp.bfloat16)
    return pl.pallas_call(
        potential_kernel,
        out_shape=(full, full),
        grid_spec=pltpu.PrefetchScalarGridSpec(
            num_scalar_prefetch=3,
            grid=(count // per,),
            in_specs=[
                pl.BlockSpec((per, pairs, slots, TILE, LANES), lambda i, *_: (i, 0, 0, 0, 0)),
                pl.BlockSpec((2, per, pairs, LANES), lambda i, *_: (0, i, 0, 0)),
            ],
            out_specs=(whole((width, width)),) * 2,
            scratch_shapes=[pltpu.VMEM((width, width), jnp.float32)] * 2,
        ),
        compiler_params=pltpu.CompilerParams(vmem_limit_bytes=VMEM_LIMIT),
        cost_estimate=pl.CostEstimate(flops=4 * chol.size, bytes_accessed=2 * chol.size, transcendentals=0),
        name="potentials",
    )(*places, chol, shifts)


def moves(orbitals, first, second):
    occupied, width = orbitals.shape
    vmem = pl.BlockSpec(memory_space=pltpu.VMEM)
    return pl.pallas_call(
        moves_kernel,
        out_shape=jax.ShapeDtypeStruct((occupied, width), jnp.bfloat16),
        in_specs=[vmem] * 3,
        out_specs=vmem,
        scratch_shapes=[pltpu.VMEM((occupied, width), jnp.bfloat16)],
        compiler_params=pltpu.CompilerParams(vmem_limit_bytes=VMEM_LIMIT),
        cost_estimate=pl.CostEstimate(
            flops=4 * occupied * width * width, bytes_accessed=4 * width * width, transcendentals=0
        ),
        name="moves",
    )(orbitals, first, second)


def spread(values, vectors):
    lead = values.shape[:-1]
    shaped = values.reshape(*lead, -1, vectors // 2, 2, 1)
    return jnp.broadcast_to(shaped, (*shaped.shape[:-1], TILE)).reshape(*shaped.shape[:-2], LANES)


def local(walkers, theta, cholesky, tiles, fields, source):
    own_walkers, occupied, width = walkers.shape
    tile_rows = width // TILE
    vectors, slots = cholesky.shape[1:3]

    halves = cholesky[0].astype(jnp.bfloat16).reshape(vectors // 2, 2, slots, TILE, TILE)
    halves = jnp.transpose(halves, (0, 2, 3, 1, 4)).reshape(vectors // 2, slots, TILE, LANES)
    count = source.shape[0]
    chol, shares = exchange(halves, walkers.reshape(count, occupied // count, width))
    chosen = jnp.take(shares, source, axis=0, mode="clip")
    origin = lax.all_to_all(chosen, "walk", split_axis=0, concat_axis=0, tiled=True)
    origin = origin.reshape(occupied, width)

    flat = tiles.reshape(-1)
    row, col = flat // tile_rows, flat % tile_rows
    places = (row * TILE, (col // 2) * LANES, col % 2)
    theta_t = theta[0].T
    drive = spread(fields[:, 0], vectors)
    bias1, shift1, orbitals = step(True, places, theta_t, walkers[0], chol, drive[0])
    bias2, shift2 = step(False, places, theta_t, orbitals, chol, drive[1])
    biases = jnp.stack([bias1, bias2])[..., ::TILE].reshape(2, 1, -1)
    own_shift = jnp.stack([shift1, shift2])[..., ::TILE].reshape(2, -1)
    all_shifts = gather_shifts(own_shift, count)
    me = lax.axis_index("walk")
    mine = lax.dynamic_index_in_dim(source, me, 0, keepdims=False)
    chosen_shift = lax.dynamic_index_in_dim(all_shifts, mine, 0, keepdims=False)
    first, second = potentials(places, chol, spread(chosen_shift, vectors), width)
    return (moves(origin, first, second)[None], biases)


def solution(mesh):
    in_specs = (
        P(("groups", "walk"), None, None),
        P(("groups", "walk"), None, None),
        P(("groups", "walk"), None, None, None),
        P("groups", None),
        P(None, ("groups", "walk"), None),
        P("groups"),
    )
    out_specs = (P(("groups", "walk"), None, None), P(None, ("groups", "walk"), None))
    return jax.shard_map(local, mesh=mesh, in_specs=in_specs, out_specs=out_specs, check_vma=False)
```

```python
import functools

import jax
import jax.numpy as jnp
from jax import lax
from jax.experimental import pallas as pl
from jax.experimental.pallas import tpu as pltpu
from jax.sharding import PartitionSpec as P

MESH = pl.DeviceIdType.MESH
TILE = 64
LANES = 128
CHUNK = 256
MIB = 1024 * 1024


def plane(count):
    chips = count // 2
    short = 1
    while (2 * short) * (2 * short) <= chips and chips % (2 * short) == 0:
        short *= 2
    return chips // short, short


def greet(count, me):
    barrier = pltpu.get_barrier_semaphore()

    @pl.loop(1, count)
    def _(k):
        pl.semaphore_signal(
            barrier, inc=1, device_id={"walk": lax.rem(me + k, count)}, device_id_type=MESH
        )

    pl.semaphore_wait(barrier, count - 1)


def exchange_kernel(count, own, rows, blocks, shares, own_sem, send, recv, row_send, row_recv):
    long, short = plane(count)
    me = lax.axis_index("walk")
    core = lax.rem(me, 2)
    y = lax.rem(me // 2, short)
    z = me // (2 * short)

    def index(a, b, c):
        return (a * short + b) * 2 + c

    parts = recv.shape[0]
    depth = own.shape[0] // parts

    def hop(source, part, slot, way, target):
        at = pl.ds(part * depth, depth)
        return pltpu.make_async_remote_copy(
            src_ref=source.at[at], dst_ref=blocks.at[slot, at], send_sem=send.at[way, part, slot],
            recv_sem=recv.at[part, slot], device_id={"walk": target}, device_id_type=MESH,
        )

    def row_copy(k):
        target = lax.rem(me + k, count)
        return pltpu.make_async_remote_copy(
            src_ref=rows.at[target], dst_ref=shares.at[me], send_sem=row_send.at[k],
            recv_sem=row_recv.at[k], device_id={"walk": target}, device_id_type=MESH,
        )

    def ways(dz, dy):
        line = dy == 0
        return (
            (0, line & (dz <= 0) & (z < long - 1), index(z + 1, y, core)),
            (1, line & (dz >= 0) & (z > 0), index(z - 1, y, core)),
            (2, (dy <= 0) & (y < short - 1), index(z, y + 1, core)),
            (3, (dy >= 0) & (y > 0), index(z, y - 1, core)),
        )

    def signed(k):
        return jnp.where(lax.rem(k, 2) == 1, (k + 1) // 2, -(k // 2))

    spread_z, spread_y = 2 * long - 1, 2 * short - 1
    greet(count, me)

    sibling = index(z, y, 1 - core)
    for part in range(parts):
        for way, whether, target in ways(0, 0):
            @pl.when(whether)
            def _(way=way, target=target):
                hop(own, part, me, way, target).start()
        hop(own, part, me, 4, sibling).start()

    keep = pltpu.make_async_copy(own, blocks.at[me], own_sem.at[0])
    keep_rows = pltpu.make_async_copy(rows.at[me], shares.at[me], own_sem.at[1])
    keep.start()
    keep_rows.start()
    row_copy(count - 1).start()

    def each(act, start):
        def body(k, seen):
            dy, dz = signed(k // spread_z), signed(lax.rem(k, spread_z))
            inside = (z + dz >= 0) & (z + dz < long) & (y + dy >= 0) & (y + dy < short)

            @pl.when(inside)
            def _():
                act(dz, dy, index(z + dz, y + dy, core), seen)

            return seen + jnp.where(inside, 1, 0)

        lax.fori_loop(start, spread_z * spread_y, body, jnp.int32(0))

    def forward(dz, dy, slot, seen):
        for part in range(parts):
            hop(own, part, slot, 0, sibling).wait_recv()
            for way, whether, target in ways(dz, dy):
                @pl.when(whether)
                def _(way=way, target=target):
                    hop(blocks.at[slot], part, slot, way, target).start()
            hop(blocks.at[slot], part, slot, 4, sibling).start()
        row_copy(2 * seen + 1).start()
        row_copy(2 * seen + 2).start()

    def finish(dz, dy, slot, seen):
        other = slot + 1 - 2 * core
        for part in range(parts):
            for way, whether, target in ways(dz, dy):
                @pl.when(whether)
                def _(way=way, target=target):
                    hop(own, part, slot, way, target).wait_send()
            hop(own, part, slot, 4, sibling).wait_send()
            hop(own, part, other, 4, sibling).wait_recv()

    each(forward, 1)
    each(finish, 0)
    keep.wait()
    keep_rows.wait()

    @pl.loop(1, count)
    def _(k):
        row_copy(k).wait()


def exchange(own, rows):
    count = rows.shape[0]
    parts = 2 if count <= 32 and own.shape[0] % 2 == 0 else 1
    anywhere = pl.BlockSpec(memory_space=pl.ANY)
    return pl.pallas_call(
        functools.partial(exchange_kernel, count),
        out_shape=(
            jax.ShapeDtypeStruct((count, *own.shape), own.dtype),
            jax.ShapeDtypeStruct(rows.shape, rows.dtype),
        ),
        in_specs=[anywhere] * 2,
        out_specs=(anywhere,) * 2,
        scratch_shapes=[
            pltpu.SemaphoreType.DMA((2,)),
            pltpu.SemaphoreType.DMA((5, parts, count)),
            pltpu.SemaphoreType.DMA((parts, count)),
            pltpu.SemaphoreType.DMA((count,)),
            pltpu.SemaphoreType.DMA((count,)),
        ],
        compiler_params=pltpu.CompilerParams(collective_id=0, has_side_effects=True),
        name="exchange",
    )(own, rows)


def shifts_kernel(count, own, every, own_sem, send, recv):
    me = lax.axis_index("walk")

    def copy(k):
        return pltpu.make_async_remote_copy(
            src_ref=own, dst_ref=every.at[me], send_sem=send.at[k], recv_sem=recv.at[k],
            device_id={"walk": lax.rem(me + k, count)}, device_id_type=MESH,
        )

    greet(count, me)

    @pl.loop(1, count)
    def _(k):
        copy(k).start()

    keep = pltpu.make_async_copy(own, every.at[me], own_sem)
    keep.start()
    keep.wait()

    @pl.loop(1, count)
    def _(k):
        copy(k).wait()


def gather_shifts(own, count):
    vmem = pl.BlockSpec(memory_space=pltpu.VMEM)
    return pl.pallas_call(
        functools.partial(shifts_kernel, count),
        out_shape=jax.ShapeDtypeStruct((count, *own.shape), own.dtype),
        in_specs=[vmem],
        out_specs=vmem,
        scratch_shapes=[
            pltpu.SemaphoreType.DMA,
            pltpu.SemaphoreType.DMA((count,)),
            pltpu.SemaphoreType.DMA((count,)),
        ],
        compiler_params=pltpu.CompilerParams(collective_id=1, has_side_effects=True),
        name="gather_shifts",
    )(own)


def half_mask(rows):
    return lax.broadcasted_iota(jnp.int32, (rows, LANES), 1) < TILE


def pick_tile(green, row, col, odd):
    chunk = green[pl.ds(pl.multiple_of(row, TILE), TILE), pl.ds(pl.multiple_of(col, LANES), LANES)]
    chunk = chunk.astype(jnp.float32)
    low = lax.broadcasted_iota(jnp.int32, chunk.shape, 1) < TILE
    keep = low == (odd == 0)
    return jnp.where(keep, chunk, pltpu.roll(chunk, TILE, 1))


def add_tile(potential, row, col, odd, shift, block):
    total = shift[0:1] * block[0].astype(jnp.float32)
    for pair in range(1, len(block)):
        total = total + shift[pair : pair + 1] * block[pair].astype(jnp.float32)
    total = total + pltpu.roll(total, TILE, 1)
    total = (0.1 * total).astype(jnp.bfloat16).astype(jnp.float32)
    low = lax.broadcasted_iota(jnp.int32, total.shape, 1) < TILE
    keep = low == (odd == 0)
    at = (pl.ds(pl.multiple_of(row, TILE), TILE), pl.ds(pl.multiple_of(col, LANES), LANES))
    potential[at] = potential[at] + jnp.where(keep, total, 0.0)


def step_kernel(move, rows_ref, cols_ref, odds_ref, theta_t, orbitals, chol, fields, *rest):
    if move:
        bias_ref, shift_ref, out, green, sums, potential = rest
    else:
        bias_ref, shift_ref, green, sums = rest
    now = pl.program_id(0)
    blocks, pairs, slots = chol.shape[:3]
    width = orbitals.shape[1]

    @pl.when(now == 0)
    def _():
        @pl.loop(0, width // CHUNK)
        def _(i):
            at = pl.ds(pl.multiple_of(i * CHUNK, CHUNK), CHUNK)
            green[:, at] = jnp.dot(
                theta_t[...], orbitals[:, at], preferred_element_type=jnp.float32
            ).astype(green.dtype)
            if move:
                potential[:, at] = jnp.zeros((potential.shape[0], CHUNK), jnp.float32)

    for b in range(blocks):
        base = (now * blocks + b) * slots
        acc = [jnp.zeros((8, LANES), jnp.float32) for _ in range(pairs)]
        for t in range(slots):
            g = pick_tile(green, rows_ref[base + t], cols_ref[base + t], odds_ref[base + t])
            for pair in range(pairs):
                product = g * chol[b, pair, t].astype(jnp.float32)
                acc[pair] = acc[pair] + jnp.sum(product.reshape(TILE // 8, 8, LANES), axis=0)
        for pair in range(pairs):
            sums[b, pair] = acc[pair]
    rows = jnp.sum(sums[...], axis=2).reshape(blocks * pairs, LANES)
    low = half_mask(blocks * pairs)
    first = jnp.sum(jnp.where(low, rows, 0.0), axis=1, keepdims=True)
    second = jnp.sum(jnp.where(low, 0.0, rows), axis=1, keepdims=True)
    bias = jnp.where(low, first, second).reshape(blocks, pairs, LANES)
    bias_ref[...] = bias
    shift_ref[...] = fields[...] - jnp.clip(0.5 * bias, -1.0, 1.0)
    if move:
        for b in range(blocks):
            base = (now * blocks + b) * slots
            shift = shift_ref[b]
            for t in range(slots):
                add_tile(
                    potential, rows_ref[base + t], cols_ref[base + t], odds_ref[base + t],
                    shift, [chol[b, pair, t] for pair in range(pairs)],
                )

    if move:
        @pl.when(now == pl.num_programs(0) - 1)
        def _():
            @pl.loop(0, width // CHUNK)
            def _(i):
                at = pl.ds(pl.multiple_of(i * CHUNK, CHUNK), CHUNK)
                moved = jnp.dot(
                    orbitals[...], potential[:, at].astype(jnp.bfloat16),
                    preferred_element_type=jnp.float32,
                )
                out[:, at] = (orbitals[:, at].astype(jnp.float32) + moved).astype(out.dtype)


def potential_kernel(rows_ref, cols_ref, odds_ref, chol, shifts, out1, out2, one, two):
    now = pl.program_id(0)
    blocks, pairs, slots = chol.shape[:3]
    width = one.shape[1]

    @pl.when(now == 0)
    def _():
        @pl.loop(0, width // CHUNK)
        def _(i):
            at = pl.ds(pl.multiple_of(i * CHUNK, CHUNK), CHUNK)
            one[:, at] = jnp.zeros((one.shape[0], CHUNK), jnp.float32)
            two[:, at] = jnp.zeros((two.shape[0], CHUNK), jnp.float32)

    @pl.loop(0, blocks)
    def _(b):
        base = (now * blocks + b) * slots
        for t in range(slots):
            block = [chol[b, pair, t] for pair in range(pairs)]
            place = (rows_ref[base + t], cols_ref[base + t], odds_ref[base + t])
            add_tile(one, *place, shifts[0, b], block)
            add_tile(two, *place, shifts[1, b], block)

    @pl.when(now == pl.num_programs(0) - 1)
    def _():
        @pl.loop(0, width // CHUNK)
        def _(i):
            at = pl.ds(pl.multiple_of(i * CHUNK, CHUNK), CHUNK)
            out1[:, at] = one[:, at].astype(out1.dtype)
            out2[:, at] = two[:, at].astype(out2.dtype)


def moves_kernel(orbitals, first, second, out, mid):
    width = orbitals.shape[1]

    def move(source, potential, target):
        @pl.loop(0, width // CHUNK)
        def _(i):
            at = pl.ds(pl.multiple_of(i * CHUNK, CHUNK), CHUNK)
            moved = jnp.dot(source[...], potential[:, at], preferred_element_type=jnp.float32)
            target[:, at] = (source[:, at].astype(jnp.float32) + moved).astype(target.dtype)

    move(orbitals, first, mid)
    move(mid, second, out)


def whole(shape):
    return pl.BlockSpec(shape, lambda i, *_: (0,) * len(shape), pipeline_mode=pl.Buffered(1))


def step(move, places, theta_t, orbitals, chol, fields):
    count, pairs, slots = chol.shape[:3]
    occupied, width = orbitals.shape
    per = 4 if count % 4 == 0 else 1
    lanes = pl.BlockSpec((per, pairs, LANES), lambda i, *_: (i, 0, 0))
    small = jax.ShapeDtypeStruct((count, pairs, LANES), jnp.float32)
    flops = 2 * occupied * width * width * (2 if move else 1)
    return pl.pallas_call(
        functools.partial(step_kernel, move),
        out_shape=(small, small) + ((jax.ShapeDtypeStruct((occupied, width), jnp.bfloat16),) if move else ()),
        grid_spec=pltpu.PrefetchScalarGridSpec(
            num_scalar_prefetch=3,
            grid=(count // per,),
            in_specs=[
                whole((width, occupied)),
                whole((occupied, width)),
                pl.BlockSpec((per, pairs, slots, TILE, LANES), lambda i, *_: (i, 0, 0, 0, 0)),
                lanes,
            ],
            out_specs=(lanes, lanes) + ((whole((occupied, width)),) if move else ()),
            scratch_shapes=[
                pltpu.VMEM((width, width), jnp.bfloat16),
                pltpu.VMEM((per, pairs, 8, LANES), jnp.float32),
            ]
            + ([pltpu.VMEM((width, width), jnp.float32)] if move else []),
        ),
        compiler_params=pltpu.CompilerParams(vmem_limit_bytes=32 * MIB),
        cost_estimate=pl.CostEstimate(flops=flops, bytes_accessed=2 * chol.size, transcendentals=0),
        name="step",
    )(*places, theta_t, orbitals, chol, fields)


def potentials(places, chol, shifts, width):
    count, pairs, slots = chol.shape[:3]
    per = 4 if count % 4 == 0 else 1
    full = jax.ShapeDtypeStruct((width, width), jnp.bfloat16)
    return pl.pallas_call(
        potential_kernel,
        out_shape=(full, full),
        grid_spec=pltpu.PrefetchScalarGridSpec(
            num_scalar_prefetch=3,
            grid=(count // per,),
            in_specs=[
                pl.BlockSpec((per, pairs, slots, TILE, LANES), lambda i, *_: (i, 0, 0, 0, 0)),
                pl.BlockSpec((2, per, pairs, LANES), lambda i, *_: (0, i, 0, 0)),
            ],
            out_specs=(whole((width, width)),) * 2,
            scratch_shapes=[pltpu.VMEM((width, width), jnp.float32)] * 2,
        ),
        compiler_params=pltpu.CompilerParams(vmem_limit_bytes=38 * MIB),
        cost_estimate=pl.CostEstimate(flops=4 * chol.size, bytes_accessed=2 * chol.size, transcendentals=0),
        name="potentials",
    )(*places, chol, shifts)


def moves(orbitals, first, second):
    occupied, width = orbitals.shape
    vmem = pl.BlockSpec(memory_space=pltpu.VMEM)
    return pl.pallas_call(
        moves_kernel,
        out_shape=jax.ShapeDtypeStruct((occupied, width), jnp.bfloat16),
        in_specs=[vmem] * 3,
        out_specs=vmem,
        scratch_shapes=[pltpu.VMEM((occupied, width), jnp.bfloat16)],
        compiler_params=pltpu.CompilerParams(vmem_limit_bytes=24 * MIB),
        cost_estimate=pl.CostEstimate(
            flops=4 * occupied * width * width, bytes_accessed=4 * width * width, transcendentals=0
        ),
        name="moves",
    )(orbitals, first, second)


def spread(values, vectors):
    lead = values.shape[:-1]
    shaped = values.reshape(*lead, -1, vectors // 2, 2, 1)
    return jnp.broadcast_to(shaped, (*shaped.shape[:-1], TILE)).reshape(*shaped.shape[:-2], LANES)


def local(walkers, theta, cholesky, tiles, fields, source):
    own_walkers, occupied, width = walkers.shape
    tile_rows = width // TILE
    vectors, slots = cholesky.shape[1:3]

    halves = cholesky[0].astype(jnp.bfloat16).reshape(vectors // 2, 2, slots, TILE, TILE)
    halves = jnp.transpose(halves, (0, 2, 3, 1, 4)).reshape(vectors // 2, slots, TILE, LANES)
    count = source.shape[0]
    chol, shares = exchange(halves, walkers.reshape(count, occupied // count, width))
    chosen = jnp.take(shares, source, axis=0, mode="clip")
    origin = lax.all_to_all(chosen, "walk", split_axis=0, concat_axis=0, tiled=True)
    origin = origin.reshape(occupied, width)

    flat = tiles.reshape(-1)
    row, col = flat // tile_rows, flat % tile_rows
    places = (row * TILE, (col // 2) * LANES, col % 2)
    theta_t = theta[0].T
    drive = spread(fields[:, 0], vectors)
    bias1, shift1, orbitals = step(True, places, theta_t, walkers[0], chol, drive[0])
    bias2, shift2 = step(False, places, theta_t, orbitals, chol, drive[1])
    biases = jnp.stack([bias1, bias2])[..., ::TILE].reshape(2, 1, -1)
    own_shift = jnp.stack([shift1, shift2])[..., ::TILE].reshape(2, -1)
    all_shifts = gather_shifts(own_shift, count)
    me = lax.axis_index("walk")
    mine = lax.dynamic_index_in_dim(source, me, 0, keepdims=False)
    chosen_shift = lax.dynamic_index_in_dim(all_shifts, mine, 0, keepdims=False)
    first, second = potentials(places, chol, spread(chosen_shift, vectors), width)
    return (moves(origin, first, second)[None], biases)


def solution(mesh):
    in_specs = (
        P(("groups", "walk"), None, None),
        P(("groups", "walk"), None, None),
        P(("groups", "walk"), None, None, None),
        P("groups", None),
        P(None, ("groups", "walk"), None),
        P("groups"),
    )
    out_specs = (P(("groups", "walk"), None, None), P(None, ("groups", "walk"), None))
    return jax.shard_map(local, mesh=mesh, in_specs=in_specs, out_specs=out_specs, check_vma=False)
```

```python
import functools

import jax
import jax.numpy as jnp
from jax import lax
from jax.experimental import pallas as pl
from jax.experimental.pallas import tpu as pltpu
from jax.sharding import PartitionSpec as P

MESH = pl.DeviceIdType.MESH
TILE = 64
LANES = 128
CHUNK = 256
MIB = 1024 * 1024


def plane(count):
    chips = count // 2
    short = 1
    while (2 * short) * (2 * short) <= chips and chips % (2 * short) == 0:
        short *= 2
    return chips // short, short


def greet(count, me):
    barrier = pltpu.get_barrier_semaphore()

    @pl.loop(1, count)
    def _(k):
        pl.semaphore_signal(
            barrier, inc=1, device_id={"walk": lax.rem(me + k, count)}, device_id_type=MESH
        )

    pl.semaphore_wait(barrier, count - 1)


def exchange_kernel(count, own, rows, blocks, shares, own_sem, send, recv, row_send, row_recv):
    long, short = plane(count)
    me = lax.axis_index("walk")
    core = lax.rem(me, 2)
    y = lax.rem(me // 2, short)
    z = me // (2 * short)

    def index(a, b, c):
        return (a * short + b) * 2 + c

    parts = recv.shape[0]
    depth = own.shape[0] // parts

    def hop(source, part, slot, way, target):
        at = pl.ds(part * depth, depth)
        return pltpu.make_async_remote_copy(
            src_ref=source.at[at], dst_ref=blocks.at[slot, at], send_sem=send.at[way, part, slot],
            recv_sem=recv.at[part, slot], device_id={"walk": target}, device_id_type=MESH,
        )

    def signed(k):
        return jnp.where(lax.rem(k, 2) == 1, (k + 1) // 2, -(k // 2))

    def row_copy(j):
        k = count // 2 + signed(j)
        target = lax.rem(me + k, count)
        return pltpu.make_async_remote_copy(
            src_ref=rows.at[target], dst_ref=shares.at[me], send_sem=row_send.at[k],
            recv_sem=row_recv.at[k], device_id={"walk": target}, device_id_type=MESH,
        )

    def ways(dz, dy):
        line = dy == 0
        return (
            (0, line & (dz <= 0) & (z < long - 1), index(z + 1, y, core)),
            (1, line & (dz >= 0) & (z > 0), index(z - 1, y, core)),
            (2, (dy <= 0) & (y < short - 1), index(z, y + 1, core)),
            (3, (dy >= 0) & (y > 0), index(z, y - 1, core)),
        )

    spread_z, spread_y = 2 * long - 1, 2 * short - 1
    greet(count, me)

    sibling = index(z, y, 1 - core)
    for part in range(parts):
        for way, whether, target in ways(0, 0):
            @pl.when(whether)
            def _(way=way, target=target):
                hop(own, part, me, way, target).start()
        hop(own, part, me, 4, sibling).start()

    keep = pltpu.make_async_copy(own, blocks.at[me], own_sem.at[0])
    keep_rows = pltpu.make_async_copy(rows.at[me], shares.at[me], own_sem.at[1])
    keep.start()
    keep_rows.start()
    batch = (count - 1) // long
    early = count - 1 - batch * (long - 1)

    @pl.loop(0, early)
    def _(j):
        row_copy(j).start()

    def each(act, start):
        def body(k, seen):
            dy, dz = signed(k // spread_z), signed(lax.rem(k, spread_z))
            inside = (z + dz >= 0) & (z + dz < long) & (y + dy >= 0) & (y + dy < short)

            @pl.when(inside)
            def _():
                act(dz, dy, index(z + dz, y + dy, core), seen)

            return seen + jnp.where(inside, 1, 0)

        lax.fori_loop(start, spread_z * spread_y, body, jnp.int32(0))

    def forward(dz, dy, slot, seen):
        for part in range(parts):
            hop(own, part, slot, 0, sibling).wait_recv()
            for way, whether, target in ways(dz, dy):
                @pl.when(whether)
                def _(way=way, target=target):
                    hop(blocks.at[slot], part, slot, way, target).start()
            hop(blocks.at[slot], part, slot, 4, sibling).start()

        @pl.when(seen < long - 1)
        def _():
            @pl.loop(0, batch)
            def _(j):
                row_copy(early + seen * batch + j).start()

    def finish(dz, dy, slot, seen):
        other = slot + 1 - 2 * core
        for part in range(parts):
            for way, whether, target in ways(dz, dy):
                @pl.when(whether)
                def _(way=way, target=target):
                    hop(own, part, slot, way, target).wait_send()
            hop(own, part, slot, 4, sibling).wait_send()
            hop(own, part, other, 4, sibling).wait_recv()

    each(forward, 1)
    each(finish, 0)
    keep.wait()
    keep_rows.wait()

    @pl.loop(0, count - 1)
    def _(j):
        row_copy(j).wait()


def exchange(own, rows):
    count = rows.shape[0]
    parts = 2 if count <= 32 and own.shape[0] % 2 == 0 else 1
    anywhere = pl.BlockSpec(memory_space=pl.ANY)
    return pl.pallas_call(
        functools.partial(exchange_kernel, count),
        out_shape=(
            jax.ShapeDtypeStruct((count, *own.shape), own.dtype),
            jax.ShapeDtypeStruct(rows.shape, rows.dtype),
        ),
        in_specs=[anywhere] * 2,
        out_specs=(anywhere,) * 2,
        scratch_shapes=[
            pltpu.SemaphoreType.DMA((2,)),
            pltpu.SemaphoreType.DMA((5, parts, count)),
            pltpu.SemaphoreType.DMA((parts, count)),
            pltpu.SemaphoreType.DMA((count,)),
            pltpu.SemaphoreType.DMA((count,)),
        ],
        compiler_params=pltpu.CompilerParams(collective_id=0, has_side_effects=True),
        name="exchange",
    )(own, rows)


def shifts_kernel(count, own, every, own_sem, send, recv):
    me = lax.axis_index("walk")

    def copy(k):
        return pltpu.make_async_remote_copy(
            src_ref=own, dst_ref=every.at[me], send_sem=send.at[k], recv_sem=recv.at[k],
            device_id={"walk": lax.rem(me + k, count)}, device_id_type=MESH,
        )

    greet(count, me)

    @pl.loop(1, count)
    def _(k):
        copy(k).start()

    keep = pltpu.make_async_copy(own, every.at[me], own_sem)
    keep.start()
    keep.wait()

    @pl.loop(1, count)
    def _(k):
        copy(k).wait()


def gather_shifts(own, count):
    vmem = pl.BlockSpec(memory_space=pltpu.VMEM)
    return pl.pallas_call(
        functools.partial(shifts_kernel, count),
        out_shape=jax.ShapeDtypeStruct((count, *own.shape), own.dtype),
        in_specs=[vmem],
        out_specs=vmem,
        scratch_shapes=[
            pltpu.SemaphoreType.DMA,
            pltpu.SemaphoreType.DMA((count,)),
            pltpu.SemaphoreType.DMA((count,)),
        ],
        compiler_params=pltpu.CompilerParams(collective_id=1, has_side_effects=True),
        name="gather_shifts",
    )(own)


def half_mask(rows):
    return lax.broadcasted_iota(jnp.int32, (rows, LANES), 1) < TILE


def pick_tile(green, row, col, odd):
    chunk = green[pl.ds(pl.multiple_of(row, TILE), TILE), pl.ds(pl.multiple_of(col, LANES), LANES)]
    chunk = chunk.astype(jnp.float32)
    low = lax.broadcasted_iota(jnp.int32, chunk.shape, 1) < TILE
    keep = low == (odd == 0)
    return jnp.where(keep, chunk, pltpu.roll(chunk, TILE, 1))


def add_tile(potential, row, col, odd, shift, block):
    total = shift[0:1] * block[0].astype(jnp.float32)
    for pair in range(1, len(block)):
        total = total + shift[pair : pair + 1] * block[pair].astype(jnp.float32)
    total = total + pltpu.roll(total, TILE, 1)
    total = (0.1 * total).astype(jnp.bfloat16).astype(jnp.float32)
    low = lax.broadcasted_iota(jnp.int32, total.shape, 1) < TILE
    keep = low == (odd == 0)
    at = (pl.ds(pl.multiple_of(row, TILE), TILE), pl.ds(pl.multiple_of(col, LANES), LANES))
    potential[at] = potential[at] + jnp.where(keep, total, 0.0)


def step_kernel(move, rows_ref, cols_ref, odds_ref, theta, orbitals, chol, fields, *rest):
    if move:
        bias_ref, shift_ref, out, green, sums, potential = rest
    else:
        bias_ref, shift_ref, green, sums = rest
    now = pl.program_id(0)
    blocks, pairs, slots = chol.shape[:3]
    width = orbitals.shape[1]

    @pl.when(now == 0)
    def _():
        @pl.loop(0, width // CHUNK)
        def _(i):
            at = pl.ds(pl.multiple_of(i * CHUNK, CHUNK), CHUNK)
            green[:, at] = lax.dot_general(
                theta[...], orbitals[:, at], (((0,), (0,)), ((), ())),
                preferred_element_type=jnp.float32,
            ).astype(green.dtype)
            if move:
                potential[:, at] = jnp.zeros((potential.shape[0], CHUNK), jnp.float32)

    for b in range(blocks):
        base = (now * blocks + b) * slots
        acc = [jnp.zeros((8, LANES), jnp.float32) for _ in range(pairs)]
        for t in range(slots):
            g = pick_tile(green, rows_ref[base + t], cols_ref[base + t], odds_ref[base + t])
            for pair in range(pairs):
                product = g * chol[b, pair, t].astype(jnp.float32)
                acc[pair] = acc[pair] + jnp.sum(product.reshape(TILE // 8, 8, LANES), axis=0)
        for pair in range(pairs):
            sums[b, pair] = acc[pair]
    rows = jnp.sum(sums[...], axis=2).reshape(blocks * pairs, LANES)
    low = half_mask(blocks * pairs)
    first = jnp.sum(jnp.where(low, rows, 0.0), axis=1, keepdims=True)
    second = jnp.sum(jnp.where(low, 0.0, rows), axis=1, keepdims=True)
    bias = jnp.where(low, first, second).reshape(blocks, pairs, LANES)
    bias_ref[...] = bias
    shift_ref[...] = fields[...] - jnp.clip(0.5 * bias, -1.0, 1.0)
    if move:
        for b in range(blocks):
            base = (now * blocks + b) * slots
            shift = shift_ref[b]
            for t in range(slots):
                add_tile(
                    potential, rows_ref[base + t], cols_ref[base + t], odds_ref[base + t],
                    shift, [chol[b, pair, t] for pair in range(pairs)],
                )

    if move:
        @pl.when(now == pl.num_programs(0) - 1)
        def _():
            @pl.loop(0, width // CHUNK)
            def _(i):
                at = pl.ds(pl.multiple_of(i * CHUNK, CHUNK), CHUNK)
                moved = jnp.dot(
                    orbitals[...], potential[:, at].astype(jnp.bfloat16),
                    preferred_element_type=jnp.float32,
                )
                out[:, at] = (orbitals[:, at].astype(jnp.float32) + moved).astype(out.dtype)


def moves_kernel(rows_ref, cols_ref, odds_ref, chol, shifts, orbitals, out, one, two, mid):
    now = pl.program_id(0)
    blocks, pairs, slots = chol.shape[:3]
    width = one.shape[1]

    @pl.when(now == 0)
    def _():
        @pl.loop(0, width // CHUNK)
        def _(i):
            at = pl.ds(pl.multiple_of(i * CHUNK, CHUNK), CHUNK)
            one[:, at] = jnp.zeros((one.shape[0], CHUNK), jnp.float32)
            two[:, at] = jnp.zeros((two.shape[0], CHUNK), jnp.float32)

    @pl.loop(0, blocks)
    def _(b):
        base = (now * blocks + b) * slots
        for t in range(slots):
            block = [chol[b, pair, t] for pair in range(pairs)]
            place = (rows_ref[base + t], cols_ref[base + t], odds_ref[base + t])
            add_tile(one, *place, shifts[0, b], block)
            add_tile(two, *place, shifts[1, b], block)

    def move(source, potential, target):
        @pl.loop(0, width // CHUNK)
        def _(i):
            at = pl.ds(pl.multiple_of(i * CHUNK, CHUNK), CHUNK)
            moved = jnp.dot(
                source[...], potential[:, at].astype(jnp.bfloat16),
                preferred_element_type=jnp.float32,
            )
            target[:, at] = (source[:, at].astype(jnp.float32) + moved).astype(target.dtype)

    @pl.when(now == pl.num_programs(0) - 1)
    def _():
        move(orbitals, one, mid)
        move(mid, two, out)


def whole(shape):
    return pl.BlockSpec(shape, lambda i, *_: (0,) * len(shape), pipeline_mode=pl.Buffered(1))


def step(move, places, theta, orbitals, chol, fields):
    count, pairs, slots = chol.shape[:3]
    occupied, width = orbitals.shape
    per = 4 if count % 4 == 0 else 1
    lanes = pl.BlockSpec((per, pairs, LANES), lambda i, *_: (i, 0, 0))
    small = jax.ShapeDtypeStruct((count, pairs, LANES), jnp.float32)
    flops = 2 * occupied * width * width * (2 if move else 1)
    return pl.pallas_call(
        functools.partial(step_kernel, move),
        out_shape=(small, small) + ((jax.ShapeDtypeStruct((occupied, width), jnp.bfloat16),) if move else ()),
        grid_spec=pltpu.PrefetchScalarGridSpec(
            num_scalar_prefetch=3,
            grid=(count // per,),
            in_specs=[
                whole((occupied, width)),
                whole((occupied, width)),
                pl.BlockSpec((per, pairs, slots, TILE, LANES), lambda i, *_: (i, 0, 0, 0, 0)),
                lanes,
            ],
            out_specs=(lanes, lanes) + ((whole((occupied, width)),) if move else ()),
            scratch_shapes=[
                pltpu.VMEM((width, width), jnp.bfloat16),
                pltpu.VMEM((per, pairs, 8, LANES), jnp.float32),
            ]
            + ([pltpu.VMEM((width, width), jnp.float32)] if move else []),
        ),
        compiler_params=pltpu.CompilerParams(vmem_limit_bytes=32 * MIB),
        cost_estimate=pl.CostEstimate(flops=flops, bytes_accessed=2 * chol.size, transcendentals=0),
        name="step",
    )(*places, theta, orbitals, chol, fields)


def moves(places, chol, shifts, orbitals):
    count, pairs, slots = chol.shape[:3]
    occupied, width = orbitals.shape
    per = 4 if count % 4 == 0 else 1
    return pl.pallas_call(
        moves_kernel,
        out_shape=jax.ShapeDtypeStruct((occupied, width), jnp.bfloat16),
        grid_spec=pltpu.PrefetchScalarGridSpec(
            num_scalar_prefetch=3,
            grid=(count // per,),
            in_specs=[
                pl.BlockSpec((per, pairs, slots, TILE, LANES), lambda i, *_: (i, 0, 0, 0, 0)),
                pl.BlockSpec((2, per, pairs, LANES), lambda i, *_: (0, i, 0, 0)),
                whole((occupied, width)),
            ],
            out_specs=whole((occupied, width)),
            scratch_shapes=[pltpu.VMEM((width, width), jnp.float32)] * 2
            + [pltpu.VMEM((occupied, width), jnp.bfloat16)],
        ),
        compiler_params=pltpu.CompilerParams(vmem_limit_bytes=38 * MIB),
        cost_estimate=pl.CostEstimate(
            flops=4 * occupied * width * width, bytes_accessed=2 * chol.size, transcendentals=0
        ),
        name="moves",
    )(*places, chol, shifts, orbitals)


def spread(values, vectors):
    lead = values.shape[:-1]
    shaped = values.reshape(*lead, -1, vectors // 2, 2, 1)
    return jnp.broadcast_to(shaped, (*shaped.shape[:-1], TILE)).reshape(*shaped.shape[:-2], LANES)


def local(walkers, theta, cholesky, tiles, fields, source):
    own_walkers, occupied, width = walkers.shape
    tile_rows = width // TILE
    vectors, slots = cholesky.shape[1:3]

    halves = cholesky[0].astype(jnp.bfloat16).reshape(vectors // 2, 2, slots, TILE, TILE)
    halves = jnp.transpose(halves, (0, 2, 3, 1, 4)).reshape(vectors // 2, slots, TILE, LANES)
    count = source.shape[0]
    chol, shares = exchange(halves, walkers.reshape(count, occupied // count, width))
    chosen = jnp.take(shares, source, axis=0, mode="clip")
    origin = lax.all_to_all(chosen, "walk", split_axis=0, concat_axis=0, tiled=True)
    origin = origin.reshape(occupied, width)

    flat = tiles.reshape(-1)
    row, col = flat // tile_rows, flat % tile_rows
    places = (row * TILE, (col // 2) * LANES, col % 2)
    drive = spread(fields[:, 0], vectors)
    bias1, shift1, orbitals = step(True, places, theta[0], walkers[0], chol, drive[0])
    bias2, shift2 = step(False, places, theta[0], orbitals, chol, drive[1])
    biases = jnp.stack([bias1, bias2])[..., ::TILE].reshape(2, 1, -1)
    own_shift = jnp.stack([shift1, shift2])[..., ::TILE].reshape(2, -1)
    all_shifts = gather_shifts(own_shift, count)
    me = lax.axis_index("walk")
    mine = lax.dynamic_index_in_dim(source, me, 0, keepdims=False)
    chosen_shift = lax.dynamic_index_in_dim(all_shifts, mine, 0, keepdims=False)
    return (moves(places, chol, spread(chosen_shift, vectors), origin)[None], biases)


def solution(mesh):
    in_specs = (
        P(("groups", "walk"), None, None),
        P(("groups", "walk"), None, None),
        P(("groups", "walk"), None, None, None),
        P("groups", None),
        P(None, ("groups", "walk"), None),
        P("groups"),
    )
    out_specs = (P(("groups", "walk"), None, None), P(None, ("groups", "walk"), None))
    return jax.shard_map(local, mesh=mesh, in_specs=in_specs, out_specs=out_specs, check_vma=False)
```
